32 devices in a mesh: dp: 8 (over y, x, core), tensor: 4 (over z).
Axes of the slice: x: 2, y: 2, z: 4, core: 2. Of those that a mesh axis runs over, the one named last changes fastest.
Arguments:
- learn_hidden: bfloat16 [384, 4096], P('dp', 'tensor'), may hold values from -360 to 360
- target_hidden: bfloat16 [384, 4096], P('dp', 'tensor'), may hold values from -360 to 360
- reward: bfloat16 [384], P('dp'), may hold values from -6 to 6
- learn_head: bfloat16 [4096, 128256], P(None, ('dp', 'tensor')), may hold values from -0.09375 to 0.09375
- target_head: bfloat16 [4096, 128256], P(None, ('dp', 'tensor')), may hold values from -0.09375 to 0.09375
- action: int32 [384], P('dp'), may hold values from 0 to 128255
- traj_len: int32 [16], P('dp'), may hold values from 1 to 24, 288 in all
- owner: int32 [16], P('dp'), may hold values from 0 to 7
Outputs:
- head_grad: bfloat16 [4096, 128256], P(None, ('dp', 'tensor'))
- hidden_grad: bfloat16 [384, 4096], P('dp', 'tensor')
- priority: float32 [8, 24], P('dp')
The draws below stay inside these ranges and needn't reach their ends.
All inputs are finite; a program needn't handle non-finite values. No bound on the sum of `traj_len` on one device may be relied on, other than what follows from the above.
Results may differ from the reference program's by a relative error of at most 0.005.
Values may be sent and summed in bfloat16 or wider, within the bound.
A program may use at most 192 MiB of HBM per device.

```python
import math
import jax
import jax.numpy as jnp
import numpy as np
from jax import lax

D = 4096
V = 128256
LEN = 24
TRAJ = 16
TOKENS = 384
OWNERS = 8


def rough_rows(key, lowest, highest):
    rows_key, cells_key = jax.random.split(key)
    cells = jnp.clip(jax.random.normal(cells_key, (TOKENS, D), jnp.float32), -6.0, 6.0)
    spread = jax.random.uniform(rows_key, (TOKENS, 1), jnp.float32, math.log(lowest), math.log(highest))
    return (cells * jnp.exp(spread)).astype(jnp.bfloat16)


def draw_learn_hidden(key, part):
    key = jax.random.fold_in(key, 11)
    return rough_rows(key, 3.0, 3.0)


def draw_target_hidden(key, part):
    key = jax.random.fold_in(key, 23)
    return rough_rows(key, 3.0, 3.0)


def with_ends(array, rng, low, top_value):
    index_at = [jax.random.randint(jax.random.fold_in(rng, axis), (), 0, length) for axis, length in enumerate(array.shape)]
    longest = array.shape.index(max(array.shape))
    next_to = index_at[:longest] + [(index_at[longest] + 1) % array.shape[longest]] + index_at[longest + 1:]
    return array.at[tuple(index_at)].set(low).at[tuple(next_to)].set(top_value)


def block_levels(stream_key, dims, shards, smallest, high):
    def one(dim, shards_of):
        steps = jax.random.uniform(jax.random.fold_in(jax.random.fold_in(stream_key, 6), dim), (shards_of,), jnp.float32, smallest / len(shards), high / len(shards))
        return jnp.repeat(jnp.exp(steps), dims[dim] // shards_of).reshape((-1,) + (1,) * (len(dims) - dim - 1))

    gain = one(*shards[0])
    for cut in shards[1:]:
        gain = gain * one(*cut)
    return gain


def wide_ids(rng, dims, number_of, lean):
    portions = [min(1 << octave, number_of + 1 - (1 << octave)) * (1 << 20) // math.isqrt((1 << octave) ** lean) + 1 for octave in range((number_of + 1).bit_length()) if 1 << octave <= number_of]
    scale = 1 + sum(portions) // (1 << 30)
    table = np.cumsum(np.array([max(1, weight // scale) for weight in portions]))
    ticket = jax.random.randint(jax.random.fold_in(rng, 1), dims, 0, int(table[len(portions) - 1]))
    start = jnp.left_shift(1, jnp.searchsorted(jnp.asarray(table, jnp.int32), ticket, side="right").astype(jnp.int32))
    standing = start - 1 + jax.random.randint(jax.random.fold_in(rng, 4), dims, 0, 1 << 30) % jnp.minimum(start, number_of + 1 - start)
    return jax.random.permutation(jax.random.fold_in(rng, 2), number_of)[standing].astype(jnp.int32)


def split_up(number_of, total, most, lean):
    weights = [(1 << 20) // math.isqrt(standing ** lean) + 1 for standing in range(2, number_of + 1)]
    rest, counts = total - most - (number_of - 1), [1] * (number_of - 1)
    while rest > 0:
        movable = [i for i in range(number_of - 1) if counts[i] < most]
        pool, remaining = sum([weights[i] for i in movable]), rest
        for i in movable:
            extra = min(most - counts[i], max(1, remaining * weights[i] // pool), rest)
            counts[i] = counts[i] + extra
            rest = rest - extra
    return np.array([most] + counts)


def ragged(stream_key, amount, total, most, skew):
    if amount == 2:
        one = jax.random.randint(stream_key, (), max(1, total - most), min(most, total - 1) + 1)
        return jnp.stack([one, total - one])
    tallies = jnp.asarray(split_up(amount, total, most, skew), jnp.int32)
    pairs = (amount - 1) // 2
    giver, receiver = tallies[1:1 + 2 * pairs:2], tallies[2:2 + 2 * pairs:2]
    margin = jnp.minimum(giver - 1, most - receiver)
    moved = jax.random.randint(jax.random.fold_in(stream_key, 1), (pairs,), 0, 1 << 20) % (margin + 1)
    tallies = tallies.at[1:1 + 2 * pairs:2].set(giver - moved).at[2:2 + 2 * pairs:2].set(receiver + moved)
    return tallies[jax.random.permutation(jax.random.fold_in(stream_key, 2), amount)]


def centred(stream_key, dims, deviation, most, cuts=(), kind=jnp.bfloat16):
    loudness = block_levels(stream_key, dims, cuts, -0.22, 0.18) if cuts else 1.0
    values = jax.random.normal(stream_key, dims, jnp.float32) * deviation * loudness
    return jnp.minimum(jnp.maximum(values, -most), most).astype(kind)


def setup_inputs(seed: int = 0) -> dict:
    keys = jax.random.split(jax.random.key(seed), 9)
    return {
        "learn_hidden": draw_learn_hidden(jax.random.fold_in(keys[8], 71), 0),
        "target_hidden": draw_target_hidden(jax.random.fold_in(keys[8], 71), 0),
        "reward": centred(keys[2], (TOKENS,), 1.0, 6.0, ((0, 8),)),
        "learn_head": centred(keys[3], (D, V), D ** -0.5, 0.09375, ((1, 32),)),
        "target_head": centred(keys[4], (D, V), D ** -0.5, 0.09375, ((1, 32),)),
        "action": with_ends(wide_ids(keys[5], (TOKENS,), V, 2), jax.random.fold_in(keys[5], 3), 0, V - 1).astype(jnp.int32),
        "traj_len": ragged(keys[6], TRAJ, TRAJ * LEN * 3 // 4, LEN, 2).astype(jnp.int32),
        "owner": with_ends(jax.random.randint(keys[7], (TRAJ,), 0, OWNERS), jax.random.fold_in(keys[7], 1), 0, OWNERS - 1).astype(jnp.int32),
    }


temper = 1.0
discount = 0.99
kl_weight = 10.0


def soft_stats(logits):
    row_max = jnp.max(logits, axis=1, keepdims=True)
    expo = jnp.exp((logits - row_max) / temper)
    total = jnp.sum(expo, axis=1, keepdims=True)
    value = row_max[:, 0] + temper * jnp.log(total[:, 0])
    return value, expo / total


def reference(learn_hidden, target_hidden, reward, learn_head, target_head, action, traj_len, owner):
    learn_q = jnp.dot(learn_hidden, learn_head, preferred_element_type=jnp.float32)
    target_q = jnp.dot(target_hidden, target_head, preferred_element_type=jnp.float32)
    learn_value, learn_p = soft_stats(learn_q)
    target_value, target_p = soft_stats(target_q)
    position = jnp.arange(TOKENS, dtype=jnp.int32)
    offset = position % LEN
    lengths = jnp.repeat(traj_len, LEN)
    live = (offset < lengths).astype(jnp.float32)
    follow = (offset + 1 < lengths).astype(jnp.float32)
    hits = action[:, None] == jnp.arange(V, dtype=jnp.int32)[None, :]
    picked = jnp.sum(jnp.where(hits, learn_q, 0.0), axis=1)
    shifted = jnp.concatenate([target_value[1:], jnp.zeros((1,), jnp.float32)])
    target_y = reward.astype(jnp.float32) + discount * follow * shifted
    delta = live * (picked - target_y)
    grad_q = (jnp.where(hits, delta[:, None], 0.0) + kl_weight * live[:, None] * (learn_p - target_p) / temper) / TRAJ
    grad_q = grad_q.astype(jnp.bfloat16)
    head_grad = lax.dot_general(learn_hidden, grad_q, (((0,), (0,)), ((), ())), preferred_element_type=jnp.float32).astype(jnp.bfloat16)
    hidden_grad = lax.dot_general(grad_q, learn_head, (((1,), (1,)), ((), ())), preferred_element_type=jnp.float32).astype(jnp.bfloat16)
    owner_table = (jnp.arange(OWNERS, dtype=jnp.int32)[:, None] == owner[None, :]).astype(jnp.float32)
    priority = jnp.dot(owner_table, jnp.abs(delta).reshape(TRAJ, LEN), precision=lax.Precision.HIGHEST)
    return head_grad, hidden_grad, priority
```

```python
import functools

import jax
import jax.numpy as jnp
from jax import lax
from jax.experimental import pallas as pl
from jax.experimental.pallas import tpu as pltpu
from jax.sharding import PartitionSpec as P

temper = 1.0
discount = 0.99
kl_weight = 10.0
MESH = pl.DeviceIdType.MESH
SEMS = pltpu.SemaphoreType.DMA


def greet(dp, tp, me, slab):
    barrier = pltpu.get_barrier_semaphore()
    for d in range(1, dp):
        pl.semaphore_signal(
            barrier, inc=1, device_id={"dp": lax.rem(me + d, dp)}, device_id_type=MESH
        )
    for d in range(1, tp):
        pl.semaphore_signal(
            barrier, inc=1, device_id={"tensor": lax.rem(slab + d, tp)}, device_id_type=MESH
        )
    pl.semaphore_wait(barrier, dp - 1 + tp - 1)


def remote(src, dst, send, recv, device):
    return pltpu.make_async_remote_copy(
        src_ref=src,
        dst_ref=dst,
        send_sem=send,
        recv_sem=recv,
        device_id=device,
        device_id_type=MESH,
    )


def gather_kernel(
    dp, tp, learn, target, small, learn_out, target_out, small_out,
    own_sem, z_send, z_recv, p_send, p_recv, c_send, c_recv, s_send, s_recv,
):
    me, slab = lax.axis_index("dp"), lax.axis_index("tensor")
    chips = dp // 2
    chip, core = me // 2, lax.rem(me, 2)
    width = learn.shape[1]
    pairs = ((learn, learn_out), (target, target_out))

    def cols(j):
        return pl.ds(pl.multiple_of(lax.rem(slab + tp - j, tp) * width, width), width)

    greet(dp, tp, me, slab)
    own = []
    for a, (x, out) in enumerate(pairs):
        own.append(pltpu.make_async_copy(x, out.at[chip, core, :, cols(0)], own_sem.at[a]))
    own.append(pltpu.make_async_copy(small, small_out.at[me], own_sem.at[2]))
    for copy in own:
        copy.start()
    sent, z, p, c, s = [], {}, {}, {}, []
    for d in range(1, dp):
        copy = remote(
            small, small_out.at[me], s_send.at[d - 1], s_recv.at[d - 1],
            {"dp": lax.rem(me + d, dp)},
        )
        copy.start()
        s.append(copy)
    for a, (x, out) in enumerate(pairs):
        for d in range(1, tp):
            z[a, d] = remote(
                x, out.at[chip, core, :, cols(0)], z_send.at[a, d - 1], z_recv.at[a, d - 1],
                {"tensor": lax.rem(slab + d, tp)},
            )
            z[a, d].start()
    for a, (x, out) in enumerate(pairs):
        for j in range(tp):
            if j:
                z[a, j].wait_recv()
            place = out.at[chip, core, :, cols(j)]
            for d in range(1, chips):
                p[a, j, d] = remote(
                    x if j == 0 else place, place, p_send.at[a, j, d - 1], p_recv.at[a, j, d - 1],
                    {"dp": lax.rem(chip + d, chips) * 2 + core},
                )
                p[a, j, d].start()
    for copy in own:
        copy.wait()
    for a, (x, out) in enumerate(pairs):
        for j in range(tp):
            for d in range(1, chips):
                p[a, j, d].wait_recv()
            place = out.at[:, core, :, cols(j)]
            c[a, j] = remote(
                place, place, c_send.at[a, j], c_recv.at[a, j], {"dp": chip * 2 + 1 - core}
            )
            c[a, j].start()
    for copy in s:
        copy.wait_recv()
    for copy in c.values():
        copy.wait_recv()
    for copy in [*s, *z.values(), *p.values(), *c.values()]:
        copy.wait_send()


def gather(dp, tp, learn, target, small):
    rows, width = learn.shape
    chips = dp // 2
    full = jax.ShapeDtypeStruct((chips, 2, rows, tp * width), learn.dtype)
    return pl.pallas_call(
        functools.partial(gather_kernel, dp, tp),
        out_shape=(full, full, jax.ShapeDtypeStruct((dp, *small.shape), small.dtype)),
        in_specs=[pl.BlockSpec(memory_space=pl.ANY)] * 3,
        out_specs=(pl.BlockSpec(memory_space=pl.ANY),) * 3,
        scratch_shapes=[
            SEMS((3,)),
            SEMS((2, tp - 1)),
            SEMS((2, tp - 1)),
            SEMS((2, tp, chips - 1)),
            SEMS((2, tp, chips - 1)),
            SEMS((2, tp)),
            SEMS((2, tp)),
            SEMS((dp - 1,)),
            SEMS((dp - 1,)),
        ],
        compiler_params=pltpu.CompilerParams(collective_id=0, has_side_effects=True),
        name="gather_hidden",
    )(learn, target, small)


def combine(buffer, count):
    parts = [buffer[i] for i in range(count)]
    rows = []
    for top in (0, 2):
        peak = parts[0][top : top + 1]
        for part in parts[1:]:
            peak = jnp.maximum(peak, part[top : top + 1])
        total = jnp.zeros_like(peak)
        for part in parts:
            total += part[top + 1 : top + 2] * jnp.exp((part[top : top + 1] - peak) / temper)
        rows += [peak, total]
    picked = jnp.zeros_like(rows[0])
    for part in parts:
        picked += part[4:5]
    rows.append(picked)
    return jnp.concatenate(rows + [jnp.zeros_like(picked)] * 3, axis=0)


def stats_kernel(dp, tp, x, out, zbuf, dbuf, z_send, z_recv, d_send, d_recv):
    me, slab = lax.axis_index("dp"), lax.axis_index("tensor")
    greet(dp, tp, me, slab)
    copies = []
    for d in range(1, tp):
        copies.append(remote(
            x, zbuf.at[slab], z_send.at[d - 1], z_recv.at[d - 1],
            {"tensor": lax.rem(slab + d, tp)},
        ))
        copies[-1].start()
    zbuf[slab] = x[...]
    for copy in copies:
        copy.wait()
    dbuf[me] = combine(zbuf, tp)
    copies = []
    for d in range(1, dp):
        copies.append(remote(
            dbuf.at[me], dbuf.at[me], d_send.at[d - 1], d_recv.at[d - 1],
            {"dp": lax.rem(me + d, dp)},
        ))
        copies[-1].start()
    for copy in copies:
        copy.wait()
    out[...] = combine(dbuf, dp)


def merge_stats(dp, tp, stats):
    vmem = pl.BlockSpec(memory_space=pltpu.VMEM)
    return pl.pallas_call(
        functools.partial(stats_kernel, dp, tp),
        out_shape=jax.ShapeDtypeStruct(stats.shape, stats.dtype),
        in_specs=[vmem],
        out_specs=vmem,
        scratch_shapes=[
            pltpu.VMEM((tp, *stats.shape), stats.dtype),
            pltpu.VMEM((dp, *stats.shape), stats.dtype),
            SEMS((tp - 1,)),
            SEMS((tp - 1,)),
            SEMS((dp - 1,)),
            SEMS((dp - 1,)),
        ],
        compiler_params=pltpu.CompilerParams(collective_id=1, has_side_effects=True),
        name="merge_stats",
    )(stats)


def scatter_kernel(
    dp, tp, part, out, crecv, csum, precv, psum, zrecv,
    c_send, c_recv, p_send, p_recv, z_send, z_recv,
):
    me, slab = lax.axis_index("dp"), lax.axis_index("tensor")
    chips = dp // 2
    chip, core = me // 2, lax.rem(me, 2)
    width = out.shape[1]

    def owner(j):
        return lax.rem(slab + 1 + j, tp)

    def cols(j):
        return pl.ds(pl.multiple_of(owner(j) * width, width), width)

    greet(dp, tp, me, slab)
    c, p, z = [], {}, []
    for j in range(tp):
        c.append(remote(
            part.at[:, 1 - core, :, cols(j)], crecv.at[:, :, cols(j)],
            c_send.at[j], c_recv.at[j], {"dp": chip * 2 + 1 - core},
        ))
        c[-1].start()
    for j in range(tp):
        c[j].wait_recv()
        for g in range(chips):
            csum[g, :, cols(j)] = (
                part[g, core, :, cols(j)].astype(jnp.float32)
                + crecv[g, :, cols(j)].astype(jnp.float32)
            ).astype(csum.dtype)
        for d in range(1, chips):
            there = lax.rem(chip + d, chips)
            p[j, d] = remote(
                csum.at[there, :, cols(j)], precv.at[d - 1, :, cols(j)],
                p_send.at[j, d - 1], p_recv.at[j, d - 1], {"dp": there * 2 + core},
            )
            p[j, d].start()
    for j in range(tp):
        total = csum[chip, :, cols(j)].astype(jnp.float32)
        for d in range(1, chips):
            p[j, d].wait_recv()
            total += precv[d - 1, :, cols(j)].astype(jnp.float32)
        if j < tp - 1:
            psum[j] = total.astype(psum.dtype)
            z.append(remote(
                psum.at[j], zrecv.at[j], z_send.at[j], z_recv.at[j], {"tensor": owner(j)}
            ))
            z[-1].start()
    for j in range(tp - 1):
        z[j].wait_recv()
        total += zrecv[j].astype(jnp.float32)
    out[...] = total.astype(out.dtype)
    for copy in [*c, *p.values(), *z]:
        copy.wait_send()


def scatter_sum(dp, tp, part):
    chips, _, rows, features = part.shape
    width = features // tp
    vmem = pl.BlockSpec(memory_space=pltpu.VMEM)
    return pl.pallas_call(
        functools.partial(scatter_kernel, dp, tp),
        out_shape=jax.ShapeDtypeStruct((rows, width), part.dtype),
        in_specs=[vmem],
        out_specs=vmem,
        scratch_shapes=[
            pltpu.VMEM((chips, rows, features), part.dtype),
            pltpu.VMEM((chips, rows, features), part.dtype),
            pltpu.VMEM((chips - 1, rows, features), part.dtype),
            pltpu.VMEM((tp - 1, rows, width), part.dtype),
            pltpu.VMEM((tp - 1, rows, width), part.dtype),
            SEMS((tp,)),
            SEMS((tp,)),
            SEMS((tp, chips - 1)),
            SEMS((tp, chips - 1)),
            SEMS((tp - 1,)),
            SEMS((tp - 1,)),
        ],
        compiler_params=pltpu.CompilerParams(
            collective_id=2, has_side_effects=True, vmem_limit_bytes=40 * 1024 * 1024
        ),
        name="scatter_sum",
    )(part)


def local_stats(logits):
    row_max = jnp.max(logits, axis=1)
    total = jnp.sum(jnp.exp((logits - row_max[:, None]) / temper), axis=1)
    return (row_max, total)


def shards(dp, tp, learn_hidden, target_hidden, reward, learn_head, target_head, action, traj_len, owner):
    rows, width = learn_hidden.shape[0], learn_head.shape[1]
    tokens, features = rows * dp, learn_hidden.shape[1] * tp
    mine = traj_len.shape[0]
    traj_count = mine * dp
    seq_len = tokens // traj_count

    def row(x):
        x = x.astype(jnp.float32)
        return jnp.pad(x, (0, 128 - x.shape[0]))

    small = jnp.concatenate(
        [jnp.stack([row(action), row(reward), row(traj_len), row(owner)]), jnp.zeros((4, 128), jnp.float32)]
    )
    learn_all, target_all, small_all = gather(dp, tp, learn_hidden, target_hidden, small)
    learn_all = learn_all.reshape(tokens, features)
    target_all = target_all.reshape(tokens, features)
    action_all = small_all[:, 0, :rows].reshape(tokens).astype(jnp.int32)
    reward_all = small_all[:, 1, :rows].reshape(tokens)
    length_all = small_all[:, 2, :mine].reshape(traj_count).astype(jnp.int32)
    owner_all = small_all[:, 3, :mine].reshape(traj_count).astype(jnp.int32)

    learn_q = jnp.dot(learn_all, learn_head, preferred_element_type=jnp.float32)
    target_q = jnp.dot(target_all, target_head, preferred_element_type=jnp.float32)
    block_index = lax.axis_index("dp") * tp + lax.axis_index("tensor")
    columns = block_index * width + jnp.arange(width, dtype=jnp.int32)
    hits = action_all[:, None] == columns[None, :]
    picked_part = jnp.sum(jnp.where(hits, learn_q, 0.0), axis=1)
    learn_peak, learn_part = local_stats(learn_q)
    target_peak, target_part = local_stats(target_q)
    blank = jnp.zeros_like(picked_part)
    merged = merge_stats(
        dp, tp,
        jnp.stack([learn_peak, learn_part, target_peak, target_part, picked_part, blank, blank, blank]),
    )
    learn_max, learn_sum, target_max, target_sum, picked = (merged[i] for i in range(5))
    target_value = target_max + temper * jnp.log(target_sum)
    learn_p = jnp.exp((learn_q - learn_max[:, None]) / temper) / learn_sum[:, None]
    target_p = jnp.exp((target_q - target_max[:, None]) / temper) / target_sum[:, None]
    position = jnp.arange(tokens, dtype=jnp.int32)
    offset = position % seq_len
    lengths = jnp.repeat(length_all, seq_len)
    live = (offset < lengths).astype(jnp.float32)
    follow = (offset + 1 < lengths).astype(jnp.float32)
    shifted = jnp.concatenate([target_value[1:], jnp.zeros((1,), jnp.float32)])
    target_y = reward_all + discount * follow * shifted
    delta = live * (picked - target_y)
    grad_q = (
        jnp.where(hits, delta[:, None], 0.0)
        + kl_weight * live[:, None] * (learn_p - target_p) / temper
    ) / traj_count
    grad_q = grad_q.astype(jnp.bfloat16)
    part = lax.dot_general(
        grad_q, learn_head, (((1,), (1,)), ((), ())), preferred_element_type=jnp.float32
    ).astype(jnp.bfloat16)
    hidden_grad = scatter_sum(dp, tp, part.reshape(dp // 2, 2, rows, features))
    head_grad = lax.dot_general(
        learn_all, grad_q, (((0,), (0,)), ((), ())), preferred_element_type=jnp.float32
    ).astype(jnp.bfloat16)
    magnitude = jnp.abs(delta).reshape(traj_count, seq_len)
    holds = (owner_all == lax.axis_index("dp")).astype(jnp.float32)
    priority = jnp.sum(holds[:, None] * magnitude, axis=0, keepdims=True)
    return (head_grad, hidden_grad, priority)


def solution(mesh):
    dp, tp = mesh.shape["dp"], mesh.shape["tensor"]
    return jax.shard_map(
        functools.partial(shards, dp, tp),
        mesh=mesh,
        in_specs=(
            P("dp", "tensor"),
            P("dp", "tensor"),
            P("dp"),
            P(None, ("dp", "tensor")),
            P(None, ("dp", "tensor")),
            P("dp"),
            P("dp"),
            P("dp"),
        ),
        out_specs=(P(None, ("dp", "tensor")), P("dp", "tensor"), P("dp", None)),
        check_vma=False,
    )
```

```python
import functools

import jax
import jax.numpy as jnp
from jax import lax
from jax.experimental import pallas as pl
from jax.experimental.pallas import tpu as pltpu
from jax.sharding import PartitionSpec as P

temper = 1.0
discount = 0.99
kl_weight = 10.0
MESH = pl.DeviceIdType.MESH
SEMS = pltpu.SemaphoreType.DMA


def greet(dp, tp, me, slab):
    barrier = pltpu.get_barrier_semaphore()
    for d in range(1, dp):
        pl.semaphore_signal(
            barrier, inc=1, device_id={"dp": lax.rem(me + d, dp)}, device_id_type=MESH
        )
    for d in range(1, tp):
        pl.semaphore_signal(
            barrier, inc=1, device_id={"tensor": lax.rem(slab + d, tp)}, device_id_type=MESH
        )
    pl.semaphore_wait(barrier, dp - 1 + tp - 1)


def remote(src, dst, send, recv, device):
    return pltpu.make_async_remote_copy(
        src_ref=src,
        dst_ref=dst,
        send_sem=send,
        recv_sem=recv,
        device_id=device,
        device_id_type=MESH,
    )


def gather_kernel(
    dp, tp, learn, target, small, learn_out, target_out, small_out,
    own_sem, z_send, z_recv, p_send, p_recv, c_send, c_recv, s_send, s_recv,
):
    me, slab = lax.axis_index("dp"), lax.axis_index("tensor")
    chips = dp // 2
    chip, core = me // 2, lax.rem(me, 2)
    width = learn.shape[1]
    pairs = ((learn, learn_out), (target, target_out))
    places = (learn_out.at[chip, core], target_out)

    def cols(j):
        return pl.ds(pl.multiple_of(lax.rem(slab + tp - j, tp) * width, width), width)

    greet(dp, tp, me, slab)
    own = []
    for a, (x, out) in enumerate(pairs):
        own.append(pltpu.make_async_copy(x, places[a].at[:, cols(0)], own_sem.at[a]))
    own.append(pltpu.make_async_copy(small, small_out.at[me], own_sem.at[2]))
    for copy in own:
        copy.start()
    sent, z, p, c, s = [], {}, {}, {}, []
    for d in range(1, dp):
        copy = remote(
            small, small_out.at[me], s_send.at[d - 1], s_recv.at[d - 1],
            {"dp": lax.rem(me + d, dp)},
        )
        copy.start()
        s.append(copy)
    for a, (x, out) in enumerate(pairs):
        for d in range(1, tp):
            z[a, d] = remote(
                x, places[a].at[:, cols(0)], z_send.at[a, d - 1], z_recv.at[a, d - 1],
                {"tensor": lax.rem(slab + d, tp)},
            )
            z[a, d].start()
    for a, (x, out) in enumerate(pairs):
        for j in range(tp):
            if j:
                z[a, j].wait_recv()
            place = places[a].at[:, cols(j)]
            for d in range(1, chips if a == 0 else 1):
                p[a, j, d] = remote(
                    x if j == 0 else place, place, p_send.at[a, j, d - 1], p_recv.at[a, j, d - 1],
                    {"dp": lax.rem(chip + d, chips) * 2 + core},
                )
                p[a, j, d].start()
    for copy in own:
        copy.wait()
    for a, (x, out) in enumerate(pairs[:1]):
        for j in range(tp):
            for d in range(1, chips):
                p[a, j, d].wait_recv()
            place = out.at[:, core, :, cols(j)]
            c[a, j] = remote(
                place, place, c_send.at[a, j], c_recv.at[a, j], {"dp": chip * 2 + 1 - core}
            )
            c[a, j].start()
    for copy in s:
        copy.wait_recv()
    for copy in c.values():
        copy.wait_recv()
    for copy in [*s, *z.values(), *p.values(), *c.values()]:
        copy.wait_send()


def gather(dp, tp, learn, target, small):
    rows, width = learn.shape
    chips = dp // 2
    full = jax.ShapeDtypeStruct((chips, 2, rows, tp * width), learn.dtype)
    line = jax.ShapeDtypeStruct((rows, tp * width), target.dtype)
    return pl.pallas_call(
        functools.partial(gather_kernel, dp, tp),
        out_shape=(full, line, jax.ShapeDtypeStruct((dp, *small.shape), small.dtype)),
        in_specs=[pl.BlockSpec(memory_space=pl.ANY)] * 3,
        out_specs=(pl.BlockSpec(memory_space=pl.ANY),) * 3,
        scratch_shapes=[
            SEMS((3,)),
            SEMS((2, tp - 1)),
            SEMS((2, tp - 1)),
            SEMS((1, tp, chips - 1)),
            SEMS((1, tp, chips - 1)),
            SEMS((1, tp)),
            SEMS((1, tp)),
            SEMS((dp - 1,)),
            SEMS((dp - 1,)),
        ],
        compiler_params=pltpu.CompilerParams(collective_id=0, has_side_effects=True),
        name="gather_hidden",
    )(learn, target, small)


def combine(buffer, count):
    parts = [buffer[i] for i in range(count)]
    rows = []
    for top in (0, 2):
        peak = parts[0][top : top + 1]
        for part in parts[1:]:
            peak = jnp.maximum(peak, part[top : top + 1])
        total = jnp.zeros_like(peak)
        for part in parts:
            total += part[top + 1 : top + 2] * jnp.exp((part[top : top + 1] - peak) / temper)
        rows += [peak, total]
    picked = jnp.zeros_like(rows[0])
    for part in parts:
        picked += part[4:5]
    rows.append(picked)
    return jnp.concatenate(rows + [jnp.zeros_like(picked)] * 3, axis=0)


def stats_kernel(dp, tp, x, out, zbuf, dbuf, z_send, z_recv, d_send, d_recv):
    me, slab = lax.axis_index("dp"), lax.axis_index("tensor")
    greet(dp, tp, me, slab)
    copies = []
    for d in range(1, tp):
        copies.append(remote(
            x, zbuf.at[slab], z_send.at[d - 1], z_recv.at[d - 1],
            {"tensor": lax.rem(slab + d, tp)},
        ))
        copies[-1].start()
    zbuf[slab] = x[...]
    for copy in copies:
        copy.wait()
    dbuf[me] = combine(zbuf, tp)
    copies = []
    for d in range(1, dp):
        copies.append(remote(
            dbuf.at[me], dbuf.at[me], d_send.at[d - 1], d_recv.at[d - 1],
            {"dp": lax.rem(me + d, dp)},
        ))
        copies[-1].start()
    for copy in copies:
        copy.wait()
    out[...] = combine(dbuf, dp)


def merge_stats(dp, tp, stats):
    vmem = pl.BlockSpec(memory_space=pltpu.VMEM)
    return pl.pallas_call(
        functools.partial(stats_kernel, dp, tp),
        out_shape=jax.ShapeDtypeStruct(stats.shape, stats.dtype),
        in_specs=[vmem],
        out_specs=vmem,
        scratch_shapes=[
            pltpu.VMEM((tp, *stats.shape), stats.dtype),
            pltpu.VMEM((dp, *stats.shape), stats.dtype),
            SEMS((tp - 1,)),
            SEMS((tp - 1,)),
            SEMS((dp - 1,)),
            SEMS((dp - 1,)),
        ],
        compiler_params=pltpu.CompilerParams(collective_id=1, has_side_effects=True),
        name="merge_stats",
    )(stats)


def cores_kernel(dp, tp, part, *refs):
    chips = dp // 2
    outs, (crecv, c_send, c_recv) = refs[:chips], refs[chips:]
    me, slab = lax.axis_index("dp"), lax.axis_index("tensor")
    chip, core = me // 2, lax.rem(me, 2)
    width = part.shape[3] // tp
    greet(dp, tp, me, slab)
    c = []
    for j in range(tp):
        cols = pl.ds(j * width, width)
        c.append(remote(
            part.at[:, 1 - core, :, cols], crecv.at[:, :, cols],
            c_send.at[j], c_recv.at[j], {"dp": chip * 2 + 1 - core},
        ))
        c[-1].start()
    for j in range(tp):
        c[j].wait_recv()
        cols = pl.ds(j * width, width)
        for d in range(chips):
            g = lax.rem(chip + d, chips)
            outs[d][:, cols] = (
                part[g, core, :, cols].astype(jnp.float32) + crecv[g, :, cols].astype(jnp.float32)
            ).astype(outs[d].dtype)
    for copy in c:
        copy.wait_send()


def slabs_kernel(dp, tp, *refs):
    chips = dp // 2
    parts, (out, psum, zrecv, z_send, z_recv) = refs[:chips], refs[chips:]
    me, slab = lax.axis_index("dp"), lax.axis_index("tensor")
    width = out.shape[1]
    greet(dp, tp, me, slab)
    z = []
    for j in range(tp):
        owner = lax.rem(slab + 1 + j, tp)
        cols = pl.ds(pl.multiple_of(owner * width, width), width)
        total = parts[0][:, cols].astype(jnp.float32)
        for part in parts[1:]:
            total += part[:, cols].astype(jnp.float32)
        if j < tp - 1:
            psum[j] = total.astype(psum.dtype)
            z.append(remote(
                psum.at[j], zrecv.at[j], z_send.at[j], z_recv.at[j], {"tensor": owner}
            ))
            z[-1].start()
    for j in range(tp - 1):
        z[j].wait_recv()
        total += zrecv[j].astype(jnp.float32)
    out[...] = total.astype(out.dtype)
    for copy in z:
        copy.wait_send()


def scatter_sum(dp, tp, part):
    chips, _, rows, features = part.shape
    width = features // tp
    vmem = pl.BlockSpec(memory_space=pltpu.VMEM)
    sums = pl.pallas_call(
        functools.partial(cores_kernel, dp, tp),
        out_shape=(jax.ShapeDtypeStruct((rows, features), part.dtype),) * chips,
        in_specs=[vmem],
        out_specs=(vmem,) * chips,
        scratch_shapes=[
            pltpu.VMEM((chips, rows, features), part.dtype),
            SEMS((tp,)),
            SEMS((tp,)),
        ],
        compiler_params=pltpu.CompilerParams(
            collective_id=2, has_side_effects=True, vmem_limit_bytes=40 * 1024 * 1024
        ),
        name="sum_cores",
    )(part)
    arrived = [sums[0]]
    for d in range(1, chips):
        route = [(i, ((i // 2 + d) % chips) * 2 + i % 2) for i in range(dp)]
        arrived.append(lax.ppermute(sums[d], "dp", route))
    return pl.pallas_call(
        functools.partial(slabs_kernel, dp, tp),
        out_shape=jax.ShapeDtypeStruct((rows, width), part.dtype),
        in_specs=[vmem] * chips,
        out_specs=vmem,
        scratch_shapes=[
            pltpu.VMEM((tp - 1, rows, width), part.dtype),
            pltpu.VMEM((tp - 1, rows, width), part.dtype),
            SEMS((tp - 1,)),
            SEMS((tp - 1,)),
        ],
        compiler_params=pltpu.CompilerParams(
            collective_id=3, has_side_effects=True, vmem_limit_bytes=40 * 1024 * 1024
        ),
        name="sum_slabs",
    )(*arrived)


def local_stats(logits):
    row_max = jnp.max(logits, axis=1)
    total = jnp.sum(jnp.exp((logits - row_max[:, None]) / temper), axis=1)
    return (row_max, total)


def shards(dp, tp, learn_hidden, target_hidden, reward, learn_head, target_head, action, traj_len, owner):
    rows, width = learn_hidden.shape[0], learn_head.shape[1]
    tokens, features = rows * dp, learn_hidden.shape[1] * tp
    mine = traj_len.shape[0]
    traj_count = mine * dp
    seq_len = tokens // traj_count

    def row(x):
        x = x.astype(jnp.float32)
        return jnp.pad(x, (0, 128 - x.shape[0]))

    small = jnp.concatenate(
        [jnp.stack([row(action), row(reward), row(traj_len), row(owner)]), jnp.zeros((4, 128), jnp.float32)]
    )
    learn_all, target_all, small_all = gather(dp, tp, learn_hidden, target_hidden, small)
    learn_all = learn_all.reshape(tokens, features)
    target_all = lax.all_gather(target_all, "dp", axis=0, tiled=True)
    action_all = small_all[:, 0, :rows].reshape(tokens).astype(jnp.int32)
    reward_all = small_all[:, 1, :rows].reshape(tokens)
    length_all = small_all[:, 2, :mine].reshape(traj_count).astype(jnp.int32)
    owner_all = small_all[:, 3, :mine].reshape(traj_count).astype(jnp.int32)

    learn_q = jnp.dot(learn_all, learn_head, preferred_element_type=jnp.float32)
    target_q = jnp.dot(target_all, target_head, preferred_element_type=jnp.float32)
    block_index = lax.axis_index("dp") * tp + lax.axis_index("tensor")
    columns = block_index * width + jnp.arange(width, dtype=jnp.int32)
    hits = action_all[:, None] == columns[None, :]
    picked_part = jnp.sum(jnp.where(hits, learn_q, 0.0), axis=1)
    learn_peak, learn_part = local_stats(learn_q)
    target_peak, target_part = local_stats(target_q)
    blank = jnp.zeros_like(picked_part)
    merged = merge_stats(
        dp, tp,
        jnp.stack([learn_peak, learn_part, target_peak, target_part, picked_part, blank, blank, blank]),
    )
    learn_max, learn_sum, target_max, target_sum, picked = (merged[i] for i in range(5))
    target_value = target_max + temper * jnp.log(target_sum)
    learn_p = jnp.exp((learn_q - learn_max[:, None]) / temper) / learn_sum[:, None]
    target_p = jnp.exp((target_q - target_max[:, None]) / temper) / target_sum[:, None]
    position = jnp.arange(tokens, dtype=jnp.int32)
    offset = position % seq_len
    lengths = jnp.repeat(length_all, seq_len)
    live = (offset < lengths).astype(jnp.float32)
    follow = (offset + 1 < lengths).astype(jnp.float32)
    shifted = jnp.concatenate([target_value[1:], jnp.zeros((1,), jnp.float32)])
    target_y = reward_all + discount * follow * shifted
    delta = live * (picked - target_y)
    grad_q = (
        jnp.where(hits, delta[:, None], 0.0)
        + kl_weight * live[:, None] * (learn_p - target_p) / temper
    ) / traj_count
    grad_q = grad_q.astype(jnp.bfloat16)
    part = lax.dot_general(
        grad_q, learn_head, (((1,), (1,)), ((), ())), preferred_element_type=jnp.float32
    ).astype(jnp.bfloat16)
    hidden_grad = scatter_sum(dp, tp, part.reshape(dp // 2, 2, rows, features))
    head_grad = lax.dot_general(
        learn_all, grad_q, (((0,), (0,)), ((), ())), preferred_element_type=jnp.float32
    ).astype(jnp.bfloat16)
    magnitude = jnp.abs(delta).reshape(traj_count, seq_len)
    holds = (owner_all == lax.axis_index("dp")).astype(jnp.float32)
    priority = jnp.sum(holds[:, None] * magnitude, axis=0, keepdims=True)
    return (head_grad, hidden_grad, priority)


def solution(mesh):
    dp, tp = mesh.shape["dp"], mesh.shape["tensor"]
    return jax.shard_map(
        functools.partial(shards, dp, tp),
        mesh=mesh,
        in_specs=(
            P("dp", "tensor"),
            P("dp", "tensor"),
            P("dp"),
            P(None, ("dp", "tensor")),
            P(None, ("dp", "tensor")),
            P("dp"),
            P("dp"),
            P("dp"),
        ),
        out_specs=(P(None, ("dp", "tensor")), P("dp", "tensor"), P("dp", None)),
        check_vma=False,
    )
```
